32 devices in a mesh: dp: 4 (over z), ctx: 2 (over x), tp: 4 (over y, core).
Axes of the slice: x: 2, y: 2, z: 4, core: 2. Of those that a mesh axis runs over, the one named last changes fastest.
Arguments:
- inputs: bfloat16 [4, 1024, 768], P('dp', ('ctx', 'tp')), may hold values from -6 to 6
- segments: int32 [4, 1024], P('dp'), may hold values from 0 to 18, as said below
- ln1_gain: bfloat16 [2, 768], P(None, 'dp'), may hold values from 0.25 to 1.75
- ln1_shift: bfloat16 [2, 768], P(None, 'dp'), may hold values from -4 to 4
- w_qkv: bfloat16 [2, 768, 3, 768], P(None, 'dp', None, 'tp'), may hold values from -0.21875 to 0.21875
- b_qv: bfloat16 [2, 2, 12, 64], P(None, None, 'tp', 'dp'), may hold values from -4 to 4
- w_out: bfloat16 [2, 768, 768], P(None, 'tp', 'dp'), may hold values from -0.875 to 0.875
- b_out: bfloat16 [2, 768], P(None, 'dp'), may hold values from -4 to 4
- ln2_gain: bfloat16 [2, 768], P(None, 'dp'), may hold values from 0.25 to 1.75
- ln2_shift: bfloat16 [2, 768], P(None, 'dp'), may hold values from -4 to 4
- w_up: bfloat16 [2, 768, 3072], P(None, 'dp', 'tp'), may hold values from -0.21875 to 0.21875
- b_up: bfloat16 [2, 48, 64], P(None, 'tp', 'dp'), may hold values from -6 to 6
- w_down: bfloat16 [2, 3072, 768], P(None, 'tp', 'dp'), may hold values from -0.109375 to 0.109375
- b_down: bfloat16 [2, 768], P(None, 'dp'), may hold values from -4 to 4
- cotangent: bfloat16 [4, 1024, 768], P('dp', ('ctx', 'tp')), may hold values from -6 to 6
Outputs:
- activations: bfloat16 [4, 1024, 768], P('dp', ('ctx', 'tp'))
- input_grad: float32 [4, 1024, 768], P('dp', ('ctx', 'tp'))
- grad_ln1_gain: float32 [2, 768], P(None, 'dp')
- grad_ln1_shift: float32 [2, 768], P(None, 'dp')
- grad_w_qkv: float32 [2, 768, 3, 768], P(None, 'dp', None, 'tp')
- grad_b_qv: float32 [2, 2, 12, 64], P(None, None, 'tp', 'dp')
- grad_w_out: float32 [2, 768, 768], P(None, 'tp', 'dp')
- grad_b_out: float32 [2, 768], P(None, 'dp')
- grad_ln2_gain: float32 [2, 768], P(None, 'dp')
- grad_ln2_shift: float32 [2, 768], P(None, 'dp')
- grad_w_up: float32 [2, 768, 3072], P(None, 'dp', 'tp')
- grad_b_up: float32 [2, 48, 64], P(None, 'tp', 'dp')
- grad_w_down: float32 [2, 3072, 768], P(None, 'tp', 'dp')
- grad_b_down: float32 [2, 768], P(None, 'dp')
The draws below stay inside these ranges and needn't reach their ends.
Inputs may be any that keep to these rules, and one draw needn't show every extreme that they name: `segments`: in each row segment numbers start at 0 and rise by one where a document begins; documents hold at most 800 tokens, all but a row's first and last at least 60; in every row one document holds both positions 511 and 512.
All inputs are finite; a program needn't handle non-finite values.
Results may differ from the reference program's by a relative error of at most 0.03.
Values may be sent and summed in bfloat16 or wider, within the bound.
A program may use at most 128 MiB of HBM per device.

```python
import jax
import jax.numpy as jnp
from jax import lax

D = 768
H = 12
FF = 3072
HD = 64
L = 2
SEQ = 1024
DOC_MIN = 60
DOC_MAX = 800
NSEQ = 4


def draw_segments(key, part):
    key = jax.random.fold_in(key, 11)
    parts_key = jax.random.split(key, 5)
    midpoint = SEQ // 2
    doc_count = SEQ // DOC_MIN + 2
    first_start = midpoint - jax.random.randint(parts_key[0], (NSEQ, 1), 1, DOC_MAX // 2 + 1)
    first_low = jnp.maximum(midpoint - first_start + DOC_MIN // 2, DOC_MIN)
    first_len = jax.random.randint(parts_key[1], (NSEQ, 1), first_low, DOC_MAX + 1)
    later_lens = jax.random.randint(parts_key[2], (NSEQ, doc_count), DOC_MIN, DOC_MAX + 1)
    earlier_lens = jax.random.randint(parts_key[3], (NSEQ, doc_count), DOC_MIN, DOC_MAX + 1)
    zero_col = jnp.zeros((NSEQ, 1), jnp.int32)
    after = first_start + first_len + jnp.concatenate([zero_col, jnp.cumsum(later_lens, axis=1).astype(jnp.int32)], axis=1)
    before = first_start - jnp.concatenate([zero_col, jnp.cumsum(earlier_lens, axis=1).astype(jnp.int32)], axis=1)
    bounds = jnp.concatenate([before, after], axis=1)
    short_first = jnp.where((midpoint - 1) % DOC_MIN == 0, 2, 1)
    short_bounds = short_first + DOC_MIN * jnp.arange(bounds.shape[1], dtype=jnp.int32)
    chosen_row = jax.random.randint(parts_key[4], (), 0, NSEQ)
    row_ids = jnp.arange(NSEQ, dtype=jnp.int32)[:, None]
    bounds = jnp.where(row_ids == chosen_row, short_bounds[None, :], bounds)
    positions = jnp.arange(SEQ, dtype=jnp.int32)
    hits = (bounds[:, None, :] <= positions[None, :, None]) & (bounds[:, None, :] > 0)
    return jnp.sum(hits.astype(jnp.int32), axis=-1).astype(jnp.int32)


def block_levels(stream_key, dims, cuts, least, high):
    def one(axis_at, blocks):
        steps = jax.random.uniform(jax.random.fold_in(jax.random.fold_in(stream_key, 6), axis_at), (blocks,), jnp.float32, least / len(cuts), high / len(cuts))
        return jnp.repeat(jnp.exp(steps), dims[axis_at] // blocks).reshape((-1,) + (1,) * (len(dims) - axis_at - 1))

    level = one(*cuts[0])
    for cut in cuts[1:]:
        level = level * one(*cut)
    return level


def noise(stream_key, shape, spread, bound, pieces=(), kind=jnp.bfloat16):
    array = jax.random.normal(stream_key, shape, jnp.float32) * spread
    if len(pieces) > 0:
        array = block_levels(stream_key, shape, pieces, -0.22, 0.18) * array
    return jnp.clip(array, min=-bound, max=bound).astype(kind)


def setup_inputs(seed: int = 0) -> dict:
    keys = jax.random.split(jax.random.key(seed), 16)
    inputs = noise(keys[0], (NSEQ, SEQ, D), 1.0, 6.0, ((0, 4), (1, 8)))
    segments = draw_segments(jax.random.fold_in(keys[15], 71), 0)
    ln1_gain = jnp.clip(1.0 + 0.15 * jax.random.normal(keys[2], (L, D), jnp.float32), 0.25, 1.75).astype(jnp.bfloat16)
    ln1_shift = noise(keys[3], (L, D), 0.3, 4.0, ((1, 4),))
    w_qkv = noise(keys[4], (L, D, 3, D), D ** -0.5, 0.21875, ((1, 4), (3, 4)))
    b_qv = noise(keys[5], (L, 2, D // 64, 64), 0.25, 4.0, ((2, 4), (3, 4)))
    w_out = noise(keys[6], (L, D, D), (D // 16) ** -0.5, 0.875, ((1, 4), (2, 4)))
    b_out = noise(keys[7], (L, D), 0.3, 4.0, ((1, 4),))
    ln2_gain = jnp.clip(1.0 + 0.15 * jax.random.normal(keys[8], (L, D), jnp.float32), 0.25, 1.75).astype(jnp.bfloat16)
    ln2_shift = noise(keys[9], (L, D), 0.3, 4.0, ((1, 4),))
    w_up = noise(keys[10], (L, D, FF), D ** -0.5, 0.21875, ((1, 4), (2, 4)))
    b_up = noise(keys[11], (L, FF // 64, 64), 0.5, 6.0, ((1, 4), (2, 4)))
    w_down = noise(keys[12], (L, FF, D), FF ** -0.5, 0.109375, ((1, 4), (2, 4)))
    b_down = noise(keys[13], (L, D), 0.3, 4.0, ((1, 4),))
    cotangent = noise(keys[14], (NSEQ, SEQ, D), 1.0, 6.0, ((0, 4), (1, 8)))
    return {"inputs": inputs, "segments": segments, "ln1_gain": ln1_gain, "ln1_shift": ln1_shift, "w_qkv": w_qkv, "b_qv": b_qv, "w_out": w_out, "b_out": b_out, "ln2_gain": ln2_gain, "ln2_shift": ln2_shift, "w_up": w_up, "b_up": b_up, "w_down": w_down, "b_down": b_down, "cotangent": cotangent}


@jax.custom_vjp
def low(v):
    return lax.optimization_barrier(v.astype(jnp.bfloat16)).astype(jnp.float32)

@jax.custom_vjp
def low_back(v):
    return v

def low_keep(v):
    return (low(v), None)

def low_pass(kept, grad):
    return (grad,)

def back_keep(v):
    return (v, None)

def back_low(kept, grad):
    return (low(grad),)
low.defvjp(low_keep, low_pass)
low_back.defvjp(back_keep, back_low)

def round_both(value):
    return low(low_back(value))

def layer_norm(stream, gain, shift):
    centered = stream - lax.optimization_barrier(jnp.mean(stream, axis=-1, keepdims=True))
    return centered * lax.rsqrt(lax.optimization_barrier(jnp.mean(centered * centered, axis=-1, keepdims=True)) + 1e-05) * gain + shift

def product(left, right):
    return jnp.dot(left, right, precision=lax.Precision.HIGHEST)

def one_layer(stream, weights, same_doc):
    gain_one, shift_one, w_qkv, b_qv, w_out, b_out, gain_two, shift_two, w_up, b_up, w_down, b_down = weights
    length = stream.shape[0]
    hidden = low(layer_norm(stream, gain_one, shift_one))
    projected = product(hidden, w_qkv.reshape(D, 3 * D)).reshape(length, 3, D)
    biases = b_qv.reshape(2, D)
    query_rows = round_both(projected[:, 0] + biases[0]).reshape(length, H, HD)
    key_rows = round_both(projected[:, 1]).reshape(length, H, HD)
    value_rows = round_both(projected[:, 2] + biases[1]).reshape(length, H, HD)
    scores = jnp.einsum('qhd,khd->hqk', query_rows, key_rows, precision=lax.Precision.HIGHEST) * HD ** (-0.5)
    scores = jnp.where(same_doc[None], low_back(scores), -1e+30)
    soft_rows = jax.nn.softmax(scores, axis=-1)
    mixed = jnp.einsum('hqk,khd->qhd', low(soft_rows), value_rows, precision=lax.Precision.HIGHEST)
    mixed = round_both(mixed.reshape(length, D))
    stream = stream + low_back(product(mixed, w_out) + b_out)
    hidden = low(layer_norm(stream, gain_two, shift_two))
    upper = low_back(product(hidden, w_up) + b_up.reshape(FF))
    stream = stream + low_back(product(low(jax.nn.gelu(upper)), w_down) + b_down)
    return stream

def forward(stream, params, same_doc):
    for layer_index in range(L):
        stream = one_layer(stream, tuple((member[layer_index] for member in params)), same_doc)
    return stream

def reference(inputs, segments, ln1_gain, ln1_shift, w_qkv, b_qv, w_out, b_out, ln2_gain, ln2_shift, w_up, b_up, w_down, b_down, cotangent):
    params = tuple((member.astype(jnp.float32) for member in (ln1_gain, ln1_shift, w_qkv, b_qv, w_out, b_out, ln2_gain, ln2_shift, w_up, b_up, w_down, b_down)))
    positions = jnp.arange(SEQ)
    causal = positions[None, :] <= positions[:, None]

    def one_sequence(totals, item):
        tokens, doc_ids, seed_grad = item
        same_doc = causal & (doc_ids[:, None] == doc_ids[None, :])
        output, pullback = jax.vjp(lambda first, second: forward(first, second, same_doc), tokens.astype(jnp.float32), params)
        token_grad, param_grads = pullback(seed_grad.astype(jnp.float32))
        totals = jax.tree.map(jnp.add, totals, param_grads)
        return (totals, (output.astype(jnp.bfloat16), token_grad))
    zeros = tuple((jnp.zeros_like(member) for member in params))
    totals, (outputs, token_grads) = lax.scan(one_sequence, zeros, (inputs, segments, cotangent))
    return (outputs, token_grads, totals[0], totals[1], totals[2], totals[3], totals[4], totals[5], totals[6], totals[7], totals[8], totals[9], totals[10], totals[11])
```

```python
import jax
import jax.numpy as jnp
from jax import lax
from jax.sharding import PartitionSpec as P

HD = 64


def shifted_2(block, axis, distance):
    devices = range(lax.axis_size(axis))
    route = [(i - distance, i) for i in devices if i - distance in devices]
    return lax.ppermute(block, axis, route)


def normalize(stream, gain, shift):
    centered = stream - jnp.mean(stream, axis=-1, keepdims=True)
    inverse = lax.rsqrt(jnp.mean(centered * centered, axis=-1, keepdims=True) + 1e-05)
    unit_rows = centered * inverse
    return (unit_rows * gain + shift, unit_rows, inverse)


def normalize_back(gradient, unit_rows, inverse, gain):
    d_unit = gradient * gain
    d_stream = inverse * (
        d_unit
        - jnp.mean(d_unit, axis=-1, keepdims=True)
        - unit_rows * jnp.mean(d_unit * unit_rows, axis=-1, keepdims=True)
    )
    return (d_stream, jnp.sum(gradient * unit_rows, axis=0), jnp.sum(gradient, axis=0))


def contract_rows(left, right):
    return lax.dot_general(
        left, right, (((0,), (0,)), ((), ())), preferred_element_type=jnp.float32
    )


def contract_cols(left, right):
    return lax.dot_general(
        left, right, (((1,), (1,)), ((), ())), preferred_element_type=jnp.float32
    )


def gather_rows(local_rows):
    return lax.all_gather(local_rows, "tp", axis=0, tiled=True)


def scatter_rows(term):
    count = lax.axis_size("tp")
    blocks = term.astype(jnp.bfloat16).reshape(count, term.shape[0] // count, term.shape[1])
    landed = lax.all_to_all(blocks, "tp", split_axis=0, concat_axis=0)
    return jnp.sum(landed.astype(jnp.float32), axis=0)


def swapped(block):
    return lax.ppermute(block, "ctx", [(0, 1), (1, 0)])


def rotated(block, distance):
    count = lax.axis_size("dp")
    return lax.ppermute(block, "dp", [(i, (i + distance) % count) for i in range(count)])


def gather_split(shard):
    count, me, side = lax.axis_size("dp"), lax.axis_index("dp"), lax.axis_index("ctx")
    rows, width = shard.shape
    half = rows // 2
    mine = lax.dynamic_slice_in_dim(shard, side * half, half)
    first = [rotated(mine, k) for k in range(1, count)]
    second = [swapped(piece) for piece in first]
    whole = jnp.zeros((count * rows, width), shard.dtype)
    whole = lax.dynamic_update_slice_in_dim(whole, shard, me * rows, 0)
    for k in range(1, count):
        base = lax.rem(me - k + count, count) * rows
        whole = lax.dynamic_update_slice_in_dim(whole, first[k - 1], base + side * half, 0)
        whole = lax.dynamic_update_slice_in_dim(whole, second[k - 1], base + (1 - side) * half, 0)
    return whole


def reduce_split(whole):
    count, me, side = lax.axis_size("dp"), lax.axis_index("dp"), lax.axis_index("ctx")
    rows, width = whole.shape[0] // count, whole.shape[1]
    half = rows // 2
    blocks = whole.reshape(count, 2, half, width)
    theirs = lax.dynamic_index_in_dim(blocks, 1 - side, 1, keepdims=False)
    mine = lax.dynamic_index_in_dim(blocks, side, 1, keepdims=False)
    both = (mine.astype(jnp.float32) + swapped(theirs).astype(jnp.float32)).astype(jnp.bfloat16)
    total = lax.dynamic_index_in_dim(both, me, 0, keepdims=False).astype(jnp.float32)
    for k in range(1, count):
        block = lax.dynamic_index_in_dim(both, lax.rem(me + k, count), 0, keepdims=False)
        total = total + rotated(block, k).astype(jnp.float32)
    total = total.astype(jnp.bfloat16)
    other = swapped(total)
    return jnp.concatenate(
        [jnp.where(side == 0, total, other), jnp.where(side == 0, other, total)], axis=0
    )


def batched(left, right, left_dim, right_dim):
    return lax.dot_general(
        left, right, (((left_dim,), (right_dim,)), ((0,), (0,))), preferred_element_type=jnp.float32
    )


def masked_scores(query_rows, key_rows, visible):
    scores = batched(query_rows, key_rows, 1, 1) * HD ** (-0.5)
    return jnp.where(visible[None], scores, -1e30)


def attend(query_rows, key_rows, value_rows, visible):
    scores = masked_scores(query_rows, key_rows, visible)
    row_max = jnp.max(scores, axis=-1)
    shifted = jnp.exp(scores - row_max[..., None])
    row_total = jnp.sum(shifted, axis=-1)
    soft_rows = (shifted / row_total[..., None]).astype(jnp.bfloat16)
    mixed = batched(value_rows, soft_rows, 2, 2)
    return (mixed, row_max + jnp.log(row_total))


def attend_back(query_rows, key_rows, value_rows, log_total, d_mixed, visible):
    scores = masked_scores(query_rows, key_rows, visible)
    soft_rows = jnp.exp(scores - log_total[..., None])
    d_soft = batched(d_mixed, value_rows, 1, 1)
    row_dot = jnp.sum(soft_rows * d_soft, axis=-1)
    d_scores = (soft_rows * (d_soft - row_dot[..., None])).astype(jnp.bfloat16)
    d_query = batched(key_rows, d_scores, 2, 2) * HD ** (-0.5)
    d_keys = batched(query_rows, d_scores, 2, 1) * HD ** (-0.5)
    d_values = batched(d_mixed, soft_rows.astype(jnp.bfloat16), 2, 1)
    return (d_query, d_keys, d_values)


def body(
    inputs,
    segments,
    ln1_gain,
    ln1_shift,
    w_qkv,
    b_qv,
    w_out,
    b_out,
    ln2_gain,
    ln2_shift,
    w_up,
    b_up,
    w_down,
    b_down,
    cotangent,
):
    tp_count = lax.axis_size("tp")
    dp_count = lax.axis_size("dp")
    pair_index = lax.axis_index("ctx")
    row_count = inputs.shape[1]
    group_rows = row_count * tp_count
    model_width = inputs.shape[2]
    layers = ln1_gain.shape[0]
    shard_rows = ln1_gain.shape[1]
    heads_width = w_qkv.shape[3]
    hidden_width = w_up.shape[2]
    head_count, head_part = b_qv.shape[2], b_qv.shape[3]
    unit_rows_up = b_up.shape[1]
    qkv_width = 3 * heads_width
    attn_width = qkv_width + heads_width
    head_shape = (heads_width // HD, HD, group_rows)
    vec_sizes = [6 * shard_rows, 2 * head_count * head_part, unit_rows_up * head_part]
    vec_total = sum(vec_sizes)
    vec_width = 128 * (-(-vec_total // (128 * shard_rows)))

    query_pos = pair_index * group_rows + jnp.arange(group_rows, dtype=jnp.int32)
    key_pos = (pair_index - 1) * group_rows + jnp.arange(2 * group_rows, dtype=jnp.int32)
    padded_ids = jnp.concatenate([jnp.full((group_rows,), -1, jnp.int32), segments[0]])
    key_ids = lax.dynamic_slice_in_dim(padded_ids, pair_index * group_rows, 2 * group_rows)
    query_ids = lax.dynamic_slice_in_dim(segments[0], pair_index * group_rows, group_rows)
    visible = (key_pos[None, :] <= query_pos[:, None]) & (key_ids[None, :] == query_ids[:, None])

    def pack_vec(rows_six, bias_qv, bias_up):
        lead = rows_six.shape[:-1]
        flat = jnp.concatenate([rows_six, bias_qv, bias_up], axis=-1)
        pad = shard_rows * vec_width - vec_total
        flat = jnp.pad(flat, [(0, 0)] * len(lead) + [(0, pad)])
        return flat.reshape(lead + (shard_rows, vec_width))

    attn_packs, mlp_packs = [], []
    for layer in range(layers):
        six = jnp.concatenate(
            [
                member[layer]
                for member in (ln1_gain, ln1_shift, b_out, ln2_gain, ln2_shift, b_down)
            ]
        )
        vec = pack_vec(six, b_qv[layer].reshape(-1), b_up[layer].reshape(-1))
        attn_packs.append(
            jnp.concatenate(
                [w_qkv[layer].reshape(shard_rows, qkv_width), w_out[layer].T, vec], axis=1
            )
        )
        mlp_packs.append(jnp.concatenate([w_up[layer], w_down[layer].T], axis=1))
    weights = []
    for layer in range(layers):
        weights.append((gather_split(attn_packs[layer]), gather_split(mlp_packs[layer])))

    stream = inputs[0].astype(jnp.float32)
    saved = []
    for layer in range(layers):
        attn_all, mlp_all = weights[layer]
        qkv_weight = attn_all[:, :qkv_width]
        out_flipped = attn_all[:, qkv_width:attn_width]
        up_weight = mlp_all[:, :hidden_width]
        down_flipped = mlp_all[:, hidden_width:]
        vecs = attn_all[:, attn_width:].reshape(dp_count, shard_rows * vec_width)
        six = (
            vecs[:, : vec_sizes[0]]
            .reshape(dp_count, 6, shard_rows)
            .swapaxes(0, 1)
            .reshape(6, model_width)
            .astype(jnp.float32)
        )
        gain_one, shift_one, out_bias, gain_two, shift_two, down_bias = [six[i] for i in range(6)]
        qv_bias = (
            vecs[:, vec_sizes[0] : vec_sizes[0] + vec_sizes[1]]
            .reshape(dp_count, 2 * head_count, head_part)
            .swapaxes(0, 1)
            .reshape(2, heads_width)
            .astype(jnp.float32)
        )
        up_bias = (
            vecs[:, vec_sizes[0] + vec_sizes[1] : vec_total]
            .reshape(dp_count, unit_rows_up, head_part)
            .swapaxes(0, 1)
            .reshape(hidden_width)
            .astype(jnp.float32)
        )
        normed, unit_one, inverse_one = normalize(stream, gain_one, shift_one)
        hidden_attn = gather_rows(normed.astype(jnp.bfloat16))
        projected = lax.dot_general(
            qkv_weight,
            hidden_attn,
            (((0,), (1,)), ((), ())),
            preferred_element_type=jnp.float32,
        ).reshape(3, heads_width, group_rows)
        query_rows = (projected[0] + qv_bias[0][:, None]).astype(jnp.bfloat16).reshape(head_shape)
        key_rows = projected[1].astype(jnp.bfloat16).reshape(head_shape)
        value_rows = (projected[2] + qv_bias[1][:, None]).astype(jnp.bfloat16).reshape(head_shape)
        earlier_keys, earlier_values = shifted_2((key_rows, value_rows), "ctx", 1)
        all_keys = jnp.concatenate([earlier_keys, key_rows], axis=2)
        all_values = jnp.concatenate([earlier_values, value_rows], axis=2)
        mixed, log_total = attend(query_rows, all_keys, all_values, visible)
        mixed = mixed.reshape(heads_width, group_rows).astype(jnp.bfloat16)
        out_term = lax.dot_general(
            mixed, out_flipped, (((0,), (1,)), ((), ())), preferred_element_type=jnp.float32
        )
        stream_mid = stream + scatter_rows(out_term) + out_bias
        normed_two, unit_two, inverse_two = normalize(stream_mid, gain_two, shift_two)
        hidden_mlp = gather_rows(normed_two.astype(jnp.bfloat16))
        upper = jnp.dot(hidden_mlp, up_weight, preferred_element_type=jnp.float32) + up_bias
        acts = jax.nn.gelu(upper).astype(jnp.bfloat16)
        stream = stream_mid + scatter_rows(contract_cols(acts, down_flipped)) + down_bias
        saved.append(
            (
                qkv_weight,
                out_flipped,
                up_weight,
                down_flipped,
                gain_one,
                gain_two,
                unit_one,
                inverse_one,
                hidden_attn,
                query_rows,
                all_keys,
                all_values,
                log_total,
                mixed,
                unit_two,
                inverse_two,
                hidden_mlp,
                upper,
                acts,
            )
        )
    gradient = cotangent[0].astype(jnp.float32)
    attn_grads, mlp_grads = [None] * layers, [None] * layers
    for layer in reversed(range(layers)):
        (
            qkv_weight,
            out_flipped,
            up_weight,
            down_flipped,
            gain_one,
            gain_two,
            unit_one,
            inverse_one,
            hidden_attn,
            query_rows,
            all_keys,
            all_values,
            log_total,
            mixed,
            unit_two,
            inverse_two,
            hidden_mlp,
            upper,
            acts,
        ) = saved[layer]
        g_mlp = gradient.astype(jnp.bfloat16)
        d_down_bias = jnp.sum(g_mlp.astype(jnp.float32), axis=0)
        wide_mlp = gather_rows(g_mlp)
        d_acts = jnp.dot(wide_mlp, down_flipped, preferred_element_type=jnp.float32)
        gelu_pull = jax.vjp(jax.nn.gelu, upper)[1]
        d_upper = gelu_pull(d_acts)[0].astype(jnp.bfloat16)
        d_norm_two = scatter_rows(contract_cols(d_upper, up_weight))
        d_up_bias = jnp.sum(d_upper.astype(jnp.float32), axis=0)
        mlp_grads[layer] = reduce_split(
            jnp.concatenate(
                [
                    contract_rows(hidden_mlp, d_upper).astype(jnp.bfloat16),
                    contract_rows(wide_mlp, acts).astype(jnp.bfloat16),
                ],
                axis=1,
            )
        )
        d_mid, d_gain_two, d_shift_two = normalize_back(d_norm_two, unit_two, inverse_two, gain_two)
        gradient_mid = gradient + d_mid
        g_attn = gradient_mid.astype(jnp.bfloat16)
        d_out_bias = jnp.sum(g_attn.astype(jnp.float32), axis=0)
        wide_attn = gather_rows(g_attn)
        d_out_flipped = lax.dot_general(
            wide_attn, mixed, (((0,), (1,)), ((), ())), preferred_element_type=jnp.float32
        ).astype(jnp.bfloat16)
        d_mixed = (
            lax.dot_general(
                out_flipped, wide_attn, (((0,), (1,)), ((), ())), preferred_element_type=jnp.float32
            )
            .astype(jnp.bfloat16)
            .reshape(head_shape)
        )
        d_query, d_keys, d_values = attend_back(
            query_rows, all_keys, all_values, log_total, d_mixed, visible
        )
        later_keys, later_values = shifted_2(
            (
                d_keys[:, :, :group_rows].astype(jnp.bfloat16),
                d_values[:, :, :group_rows].astype(jnp.bfloat16),
            ),
            "ctx",
            -1,
        )
        d_query = d_query.astype(jnp.bfloat16).reshape(heads_width, group_rows)
        d_key_own = (
            (d_keys[:, :, group_rows:] + later_keys.astype(jnp.float32))
            .astype(jnp.bfloat16)
            .reshape(heads_width, group_rows)
        )
        d_value_own = (
            (d_values[:, :, group_rows:] + later_values.astype(jnp.float32))
            .astype(jnp.bfloat16)
            .reshape(heads_width, group_rows)
        )
        d_projected = jnp.concatenate([d_query, d_key_own, d_value_own], axis=0)
        d_norm_one = scatter_rows(
            lax.dot_general(
                d_projected, qkv_weight, (((0,), (1,)), ((), ())), preferred_element_type=jnp.float32
            )
        )
        d_qkv_weight = lax.dot_general(
            hidden_attn, d_projected, (((0,), (1,)), ((), ())), preferred_element_type=jnp.float32
        ).astype(jnp.bfloat16)
        d_qv_bias = jnp.stack(
            [
                jnp.sum(d_query.astype(jnp.float32), axis=1),
                jnp.sum(d_value_own.astype(jnp.float32), axis=1),
            ]
        )
        d_input, d_gain_one, d_shift_one = normalize_back(
            d_norm_one, unit_one, inverse_one, gain_one
        )
        gradient = gradient_mid + d_input
        six = jnp.stack(
            [d_gain_one, d_shift_one, d_out_bias, d_gain_two, d_shift_two, d_down_bias]
        ).reshape(6, dp_count, shard_rows)
        vec = pack_vec(
            six.swapaxes(0, 1).reshape(dp_count, -1),
            d_qv_bias.reshape(2 * head_count, dp_count, head_part)
            .swapaxes(0, 1)
            .reshape(dp_count, -1),
            d_up_bias.reshape(unit_rows_up, dp_count, head_part)
            .swapaxes(0, 1)
            .reshape(dp_count, -1),
        )
        attn_grads[layer] = reduce_split(
            jnp.concatenate(
                [
                    d_qkv_weight,
                    d_out_flipped,
                    vec.reshape(model_width, vec_width).astype(jnp.bfloat16),
                ],
                axis=1,
            )
        )
    attn_grad = jnp.stack(attn_grads).astype(jnp.float32)
    mlp_grad = jnp.stack(mlp_grads).astype(jnp.float32)
    vec = attn_grad[:, :, attn_width:].reshape(layers, -1)
    six = jnp.sum(lax.all_gather(vec[:, : vec_sizes[0]], "tp", axis=0, tiled=False), axis=0)
    six = six.reshape(layers, 6, shard_rows)
    edge = vec_sizes[0] + vec_sizes[1]
    return (
        stream.astype(jnp.bfloat16)[None],
        gradient[None],
        six[:, 0],
        six[:, 1],
        attn_grad[:, :, :qkv_width].reshape(w_qkv.shape),
        vec[:, vec_sizes[0] : edge].reshape(b_qv.shape),
        attn_grad[:, :, qkv_width:attn_width].swapaxes(1, 2),
        six[:, 2],
        six[:, 3],
        six[:, 4],
        mlp_grad[:, :, :hidden_width],
        vec[:, edge:vec_total].reshape(b_up.shape),
        mlp_grad[:, :, hidden_width:].swapaxes(1, 2),
        six[:, 5],
    )


def solution(mesh):
    in_specs = (
        P("dp", ("ctx", "tp"), None),
        P("dp", None),
        P(None, "dp"),
        P(None, "dp"),
        P(None, "dp", None, "tp"),
        P(None, None, "tp", "dp"),
        P(None, "tp", "dp"),
        P(None, "dp"),
        P(None, "dp"),
        P(None, "dp"),
        P(None, "dp", "tp"),
        P(None, "tp", "dp"),
        P(None, "tp", "dp"),
        P(None, "dp"),
        P("dp", ("ctx", "tp"), None),
    )
    out_specs = (
        P("dp", ("ctx", "tp"), None),
        P("dp", ("ctx", "tp"), None),
        P(None, "dp"),
        P(None, "dp"),
        P(None, "dp", None, "tp"),
        P(None, None, "tp", "dp"),
        P(None, "tp", "dp"),
        P(None, "dp"),
        P(None, "dp"),
        P(None, "dp"),
        P(None, "dp", "tp"),
        P(None, "tp", "dp"),
        P(None, "tp", "dp"),
        P(None, "dp"),
    )
    return jax.shard_map(body, mesh=mesh, in_specs=in_specs, out_specs=out_specs, check_vma=False)
```

```python
import functools

import jax
import jax.numpy as jnp
from jax import lax
from jax.experimental import pallas as pl
from jax.experimental.pallas import tpu as pltpu
from jax.sharding import PartitionSpec as P

HD = 64


def shifted_2(block, axis, distance):
    devices = range(lax.axis_size(axis))
    route = [(i - distance, i) for i in devices if i - distance in devices]
    return lax.ppermute(block, axis, route)


def normalize(stream, gain, shift):
    centered = stream - jnp.mean(stream, axis=-1, keepdims=True)
    inverse = lax.rsqrt(jnp.mean(centered * centered, axis=-1, keepdims=True) + 1e-05)
    unit_rows = centered * inverse
    return (unit_rows * gain + shift, unit_rows, inverse)


def normalize_back(gradient, unit_rows, inverse, gain):
    d_unit = gradient * gain
    d_stream = inverse * (
        d_unit
        - jnp.mean(d_unit, axis=-1, keepdims=True)
        - unit_rows * jnp.mean(d_unit * unit_rows, axis=-1, keepdims=True)
    )
    return (d_stream, jnp.sum(gradient * unit_rows, axis=0), jnp.sum(gradient, axis=0))


def contract_rows(left, right):
    return lax.dot_general(
        left, right, (((0,), (0,)), ((), ())), preferred_element_type=jnp.float32
    )


def contract_cols(left, right):
    return lax.dot_general(
        left, right, (((1,), (1,)), ((), ())), preferred_element_type=jnp.float32
    )


def gather_rows(local_rows):
    return lax.all_gather(local_rows, "tp", axis=0, tiled=True)


def scatter_rows(term):
    count = lax.axis_size("tp")
    blocks = term.astype(jnp.bfloat16).reshape(count, term.shape[0] // count, term.shape[1])
    landed = lax.all_to_all(blocks, "tp", split_axis=0, concat_axis=0)
    return jnp.sum(landed.astype(jnp.float32), axis=0)


def swapped(block):
    return lax.ppermute(block, "ctx", [(0, 1), (1, 0)])


def rotated(block, distance):
    count = lax.axis_size("dp")
    return lax.ppermute(block, "dp", [(i, (i + distance) % count) for i in range(count)])


def gather_kernel(count, pieces, *refs):
    ins, outs = refs[:pieces], refs[pieces : 2 * pieces]
    line_send, line_recv, side_send, side_recv, own_sem = refs[2 * pieces :]
    me, side = lax.axis_index("dp"), lax.axis_index("ctx")
    barrier = pltpu.get_barrier_semaphore()
    pl.semaphore_signal(
        barrier, inc=1, device_id={"ctx": 1 - side}, device_id_type=pl.DeviceIdType.MESH
    )
    for way in (1, -1):

        @pl.when((me + way >= 0) & (me + way < count))
        def _():
            pl.semaphore_signal(
                barrier, inc=1, device_id={"dp": me + way}, device_id_type=pl.DeviceIdType.MESH
            )

    ends = jnp.where(me == 0, 1, 0) + jnp.where(me == count - 1, 1, 0)
    pl.semaphore_wait(barrier, 3 - ends)

    def line(piece, turn, step):
        way = 1 - 2 * turn
        owner = me - way * (step - 1)
        source = ins[piece].at[side] if step == 1 else outs[piece].at[owner, side]
        return pltpu.make_async_remote_copy(
            src_ref=source,
            dst_ref=outs[piece].at[owner, side],
            send_sem=line_send.at[piece, turn, step - 1],
            recv_sem=line_recv.at[piece, turn, step - 1],
            device_id={"dp": me + way},
            device_id_type=pl.DeviceIdType.MESH,
        )

    def arriving(piece, turn, step):
        owner = me - (1 - 2 * turn) * step
        return pltpu.make_async_remote_copy(
            src_ref=ins[piece].at[side],
            dst_ref=outs[piece].at[owner, side],
            send_sem=line_send.at[piece, turn, step - 1],
            recv_sem=line_recv.at[piece, turn, step - 1],
            device_id={"ctx": 1 - side},
            device_id_type=pl.DeviceIdType.MESH,
        )

    def across(piece, turn, step, half):
        owner = me - (1 - 2 * turn) * step
        return pltpu.make_async_remote_copy(
            src_ref=outs[piece].at[owner, half],
            dst_ref=outs[piece].at[owner, half],
            send_sem=side_send.at[piece, turn, step - 1],
            recv_sem=side_recv.at[piece, turn, step - 1],
            device_id={"ctx": 1 - side},
            device_id_type=pl.DeviceIdType.MESH,
        )

    def sends(turn, step):
        way = 1 - 2 * turn
        owner = me - way * (step - 1)
        return (owner >= 0) & (owner < count) & (me + way >= 0) & (me + way < count)

    def lands(turn, step):
        owner = me - (1 - 2 * turn) * step
        return (owner >= 0) & (owner < count)

    def own(piece):
        return pltpu.make_async_copy(ins[piece], outs[piece].at[me], own_sem.at[piece])

    for piece in range(pieces):
        for turn in (0, 1):

            @pl.when(sends(turn, 1))
            def _():
                line(piece, turn, 1).start()

    for piece in range(pieces):
        own(piece).start()
    for step in range(1, count):
        for piece in range(pieces):
            for turn in (0, 1):

                @pl.when(lands(turn, step))
                def _():
                    arriving(piece, turn, step).wait_recv()
                    across(piece, turn, step, side).start()

                if step + 1 < count:

                    @pl.when(sends(turn, step + 1))
                    def _():
                        line(piece, turn, step + 1).start()

    for step in range(1, count):
        for piece in range(pieces):
            for turn in (0, 1):

                @pl.when(lands(turn, step))
                def _():
                    across(piece, turn, step, side).wait_send()
                    across(piece, turn, step, 1 - side).wait_recv()

                @pl.when(sends(turn, step))
                def _():
                    line(piece, turn, step).wait_send()

    for piece in range(pieces):
        own(piece).wait()


def gather_shards(shards):
    count = lax.axis_size("dp")
    pieces = len(shards)
    padded = []
    for shard in shards:
        pad = -shard.shape[0] % 32
        shard = jnp.pad(shard, ((0, pad), (0, 0))) if pad else shard
        padded.append(shard.reshape(2, shard.shape[0] // 2, shard.shape[1]))
    steps = (pieces, 2, max(count - 1, 1))
    landed = pl.pallas_call(
        functools.partial(gather_kernel, count, pieces),
        out_shape=[jax.ShapeDtypeStruct((count,) + item.shape, item.dtype) for item in padded],
        in_specs=[pl.BlockSpec(memory_space=pl.ANY)] * pieces,
        out_specs=[pl.BlockSpec(memory_space=pl.ANY)] * pieces,
        scratch_shapes=[pltpu.SemaphoreType.DMA(steps)] * 4 + [pltpu.SemaphoreType.DMA((pieces,))],
        compiler_params=pltpu.CompilerParams(collective_id=0, has_side_effects=True),
    )(*padded)
    return [
        item.reshape(count, -1, item.shape[-1])[:, : shard.shape[0]]
        for item, shard in zip(landed, shards)
    ]


def reduce_split(whole):
    count, me, side = lax.axis_size("dp"), lax.axis_index("dp"), lax.axis_index("ctx")
    rows, width = whole.shape[0] // count, whole.shape[1]
    half = rows // 2
    blocks = whole.reshape(count, 2, half, width)
    theirs = lax.dynamic_index_in_dim(blocks, 1 - side, 1, keepdims=False)
    mine = lax.dynamic_index_in_dim(blocks, side, 1, keepdims=False)
    both = (mine.astype(jnp.float32) + swapped(theirs).astype(jnp.float32)).astype(jnp.bfloat16)
    total = lax.dynamic_index_in_dim(both, me, 0, keepdims=False).astype(jnp.float32)
    for k in range(1, count):
        block = lax.dynamic_index_in_dim(both, lax.rem(me + k, count), 0, keepdims=False)
        total = total + rotated(block, k).astype(jnp.float32)
    total = total.astype(jnp.bfloat16)
    other = swapped(total)
    return jnp.concatenate(
        [jnp.where(side == 0, total, other), jnp.where(side == 0, other, total)], axis=0
    )


def batched(left, right, left_dim, right_dim):
    return lax.dot_general(
        left, right, (((left_dim,), (right_dim,)), ((0,), (0,))), preferred_element_type=jnp.float32
    )


def masked_scores(query_rows, key_rows, visible):
    scores = batched(query_rows, key_rows, 1, 1) * HD ** (-0.5)
    return jnp.where(visible[None], scores, -1e30)


def attend(query_rows, key_rows, value_rows, visible):
    scores = masked_scores(query_rows, key_rows, visible)
    row_max = jnp.max(scores, axis=-1)
    shifted = jnp.exp(scores - row_max[..., None])
    row_total = jnp.sum(shifted, axis=-1)
    soft_rows = (shifted / row_total[..., None]).astype(jnp.bfloat16)
    mixed = batched(value_rows, soft_rows, 2, 2)
    return (mixed, row_max + jnp.log(row_total))


def attend_back(query_rows, key_rows, value_rows, log_total, d_mixed, visible):
    scores = masked_scores(query_rows, key_rows, visible)
    soft_rows = jnp.exp(scores - log_total[..., None])
    d_soft = batched(d_mixed, value_rows, 1, 1)
    row_dot = jnp.sum(soft_rows * d_soft, axis=-1)
    d_scores = (soft_rows * (d_soft - row_dot[..., None])).astype(jnp.bfloat16)
    d_query = batched(key_rows, d_scores, 2, 2) * HD ** (-0.5)
    d_keys = batched(query_rows, d_scores, 2, 1) * HD ** (-0.5)
    d_values = batched(d_mixed, soft_rows.astype(jnp.bfloat16), 2, 1)
    return (d_query, d_keys, d_values)


def body(
    inputs,
    segments,
    ln1_gain,
    ln1_shift,
    w_qkv,
    b_qv,
    w_out,
    b_out,
    ln2_gain,
    ln2_shift,
    w_up,
    b_up,
    w_down,
    b_down,
    cotangent,
):
    tp_count = lax.axis_size("tp")
    dp_count = lax.axis_size("dp")
    pair_index = lax.axis_index("ctx")
    row_count = inputs.shape[1]
    group_rows = row_count * tp_count
    model_width = inputs.shape[2]
    layers = ln1_gain.shape[0]
    shard_rows = ln1_gain.shape[1]
    heads_width = w_qkv.shape[3]
    hidden_width = w_up.shape[2]
    head_count, head_part = b_qv.shape[2], b_qv.shape[3]
    unit_rows_up = b_up.shape[1]
    qkv_width = 3 * heads_width
    attn_width = qkv_width + heads_width
    head_shape = (heads_width // HD, HD, group_rows)
    vec_sizes = [6 * shard_rows, 2 * head_count * head_part, unit_rows_up * head_part]
    vec_total = sum(vec_sizes)
    vec_width = 128 * (-(-vec_total // (128 * shard_rows)))

    query_pos = pair_index * group_rows + jnp.arange(group_rows, dtype=jnp.int32)
    key_pos = (pair_index - 1) * group_rows + jnp.arange(2 * group_rows, dtype=jnp.int32)
    padded_ids = jnp.concatenate([jnp.full((group_rows,), -1, jnp.int32), segments[0]])
    key_ids = lax.dynamic_slice_in_dim(padded_ids, pair_index * group_rows, 2 * group_rows)
    query_ids = lax.dynamic_slice_in_dim(segments[0], pair_index * group_rows, group_rows)
    visible = (key_pos[None, :] <= query_pos[:, None]) & (key_ids[None, :] == query_ids[:, None])

    def pack_vec(rows_six, bias_qv, bias_up):
        lead = rows_six.shape[:-1]
        flat = jnp.concatenate([rows_six, bias_qv, bias_up], axis=-1)
        pad = shard_rows * vec_width - vec_total
        flat = jnp.pad(flat, [(0, 0)] * len(lead) + [(0, pad)])
        return flat.reshape(lead + (shard_rows, vec_width))

    shards = []
    for layer in range(layers):
        shards.append(
            jnp.concatenate(
                [w_qkv[layer].reshape(shard_rows, qkv_width), w_out[layer].T], axis=1
            )
        )
        shards.append(jnp.concatenate([w_up[layer], w_down[layer].T], axis=1))
    side_width = 128 * (-(-max(shard_rows, head_part) // 128))
    vec_rows = []
    for member in (ln1_gain, ln1_shift, b_out, ln2_gain, ln2_shift, b_down, b_qv, b_up):
        flat = member.reshape(-1, member.shape[-1])
        vec_rows.append(jnp.pad(flat, ((0, 0), (0, side_width - flat.shape[1]))))
    shards.append(jnp.concatenate(vec_rows, axis=0))
    landed = gather_shards(shards)
    vecs = landed[-1].astype(jnp.float32)
    edge_six, edge_qv = 6 * layers, 6 * layers + 2 * layers * head_count

    def widened(start, stop, width):
        return jnp.concatenate([vecs[i, start:stop, :width] for i in range(dp_count)], axis=1)

    all_six = widened(0, edge_six, shard_rows)
    all_qv = widened(edge_six, edge_qv, head_part).reshape(layers, 2, head_count, HD)
    all_up = widened(edge_qv, edge_qv + layers * unit_rows_up, head_part)
    all_up = all_up.reshape(layers, hidden_width)

    stream = inputs[0].astype(jnp.float32)
    saved = []
    for layer in range(layers):
        attn_all = landed[2 * layer].reshape(model_width, attn_width)
        mlp_all = landed[2 * layer + 1].reshape(model_width, 2 * hidden_width)
        qkv_weight = attn_all[:, :qkv_width]
        out_flipped = attn_all[:, qkv_width:attn_width]
        up_weight = mlp_all[:, :hidden_width]
        down_flipped = mlp_all[:, hidden_width:]
        gain_one, shift_one, out_bias, gain_two, shift_two, down_bias = [
            all_six[member * layers + layer] for member in range(6)
        ]
        up_bias = all_up[layer]
        normed, unit_one, inverse_one = normalize(stream, gain_one, shift_one)
        hidden_attn = gather_rows(normed.astype(jnp.bfloat16))
        projected = lax.dot_general(
            qkv_weight,
            hidden_attn,
            (((0,), (1,)), ((), ())),
            preferred_element_type=jnp.float32,
        ).reshape((3,) + head_shape)
        query_rows = (projected[0] + all_qv[layer, 0][:, :, None]).astype(jnp.bfloat16)
        key_rows = projected[1].astype(jnp.bfloat16)
        value_rows = (projected[2] + all_qv[layer, 1][:, :, None]).astype(jnp.bfloat16)
        earlier_keys, earlier_values = shifted_2((key_rows, value_rows), "ctx", 1)
        all_keys = jnp.concatenate([earlier_keys, key_rows], axis=2)
        all_values = jnp.concatenate([earlier_values, value_rows], axis=2)
        mixed, log_total = attend(query_rows, all_keys, all_values, visible)
        mixed = mixed.reshape(heads_width, group_rows).astype(jnp.bfloat16)
        out_term = lax.dot_general(
            mixed, out_flipped, (((0,), (1,)), ((), ())), preferred_element_type=jnp.float32
        )
        stream_mid = stream + scatter_rows(out_term) + out_bias
        normed_two, unit_two, inverse_two = normalize(stream_mid, gain_two, shift_two)
        hidden_mlp = gather_rows(normed_two.astype(jnp.bfloat16))
        upper = jnp.dot(hidden_mlp, up_weight, preferred_element_type=jnp.float32) + up_bias
        acts = jax.nn.gelu(upper).astype(jnp.bfloat16)
        stream = stream_mid + scatter_rows(contract_cols(acts, down_flipped)) + down_bias
        saved.append(
            (
                qkv_weight,
                out_flipped,
                up_weight,
                down_flipped,
                gain_one,
                gain_two,
                unit_one,
                inverse_one,
                hidden_attn,
                query_rows,
                all_keys,
                all_values,
                log_total,
                mixed,
                unit_two,
                inverse_two,
                hidden_mlp,
                upper,
                acts,
            )
        )
    gradient = cotangent[0].astype(jnp.float32)
    attn_grads, mlp_grads = [None] * layers, [None] * layers
    for layer in reversed(range(layers)):
        (
            qkv_weight,
            out_flipped,
            up_weight,
            down_flipped,
            gain_one,
            gain_two,
            unit_one,
            inverse_one,
            hidden_attn,
            query_rows,
            all_keys,
            all_values,
            log_total,
            mixed,
            unit_two,
            inverse_two,
            hidden_mlp,
            upper,
            acts,
        ) = saved[layer]
        g_mlp = gradient.astype(jnp.bfloat16)
        d_down_bias = jnp.sum(g_mlp.astype(jnp.float32), axis=0)
        wide_mlp = gather_rows(g_mlp)
        d_acts = jnp.dot(wide_mlp, down_flipped, preferred_element_type=jnp.float32)
        gelu_pull = jax.vjp(jax.nn.gelu, upper)[1]
        d_upper = gelu_pull(d_acts)[0].astype(jnp.bfloat16)
        d_norm_two = scatter_rows(contract_cols(d_upper, up_weight))
        d_up_bias = jnp.sum(d_upper.astype(jnp.float32), axis=0)
        mlp_grads[layer] = reduce_split(
            jnp.concatenate(
                [
                    contract_rows(hidden_mlp, d_upper).astype(jnp.bfloat16),
                    contract_rows(wide_mlp, acts).astype(jnp.bfloat16),
                ],
                axis=1,
            )
        )
        d_mid, d_gain_two, d_shift_two = normalize_back(d_norm_two, unit_two, inverse_two, gain_two)
        gradient_mid = gradient + d_mid
        g_attn = gradient_mid.astype(jnp.bfloat16)
        d_out_bias = jnp.sum(g_attn.astype(jnp.float32), axis=0)
        wide_attn = gather_rows(g_attn)
        d_out_flipped = lax.dot_general(
            wide_attn, mixed, (((0,), (1,)), ((), ())), preferred_element_type=jnp.float32
        ).astype(jnp.bfloat16)
        d_mixed = (
            lax.dot_general(
                out_flipped, wide_attn, (((0,), (1,)), ((), ())), preferred_element_type=jnp.float32
            )
            .astype(jnp.bfloat16)
            .reshape(head_shape)
        )
        d_query, d_keys, d_values = attend_back(
            query_rows, all_keys, all_values, log_total, d_mixed, visible
        )
        later_keys, later_values = shifted_2(
            (
                d_keys[:, :, :group_rows].astype(jnp.bfloat16),
                d_values[:, :, :group_rows].astype(jnp.bfloat16),
            ),
            "ctx",
            -1,
        )
        d_query = d_query.astype(jnp.bfloat16).reshape(heads_width, group_rows)
        d_key_own = (
            (d_keys[:, :, group_rows:] + later_keys.astype(jnp.float32))
            .astype(jnp.bfloat16)
            .reshape(heads_width, group_rows)
        )
        d_value_own = (
            (d_values[:, :, group_rows:] + later_values.astype(jnp.float32))
            .astype(jnp.bfloat16)
            .reshape(heads_width, group_rows)
        )
        d_projected = jnp.concatenate([d_query, d_key_own, d_value_own], axis=0)
        d_norm_one = scatter_rows(
            lax.dot_general(
                d_projected, qkv_weight, (((0,), (1,)), ((), ())), preferred_element_type=jnp.float32
            )
        )
        d_qkv_weight = lax.dot_general(
            hidden_attn, d_projected, (((0,), (1,)), ((), ())), preferred_element_type=jnp.float32
        ).astype(jnp.bfloat16)
        d_qv_bias = jnp.stack(
            [
                jnp.sum(d_query.astype(jnp.float32), axis=1),
                jnp.sum(d_value_own.astype(jnp.float32), axis=1),
            ]
        )
        d_input, d_gain_one, d_shift_one = normalize_back(
            d_norm_one, unit_one, inverse_one, gain_one
        )
        gradient = gradient_mid + d_input
        six = jnp.stack(
            [d_gain_one, d_shift_one, d_out_bias, d_gain_two, d_shift_two, d_down_bias]
        ).reshape(6, dp_count, shard_rows)
        vec = pack_vec(
            six.swapaxes(0, 1).reshape(dp_count, -1),
            d_qv_bias.reshape(2 * head_count, dp_count, head_part)
            .swapaxes(0, 1)
            .reshape(dp_count, -1),
            d_up_bias.reshape(unit_rows_up, dp_count, head_part)
            .swapaxes(0, 1)
            .reshape(dp_count, -1),
        )
        attn_grads[layer] = reduce_split(
            jnp.concatenate(
                [
                    d_qkv_weight,
                    d_out_flipped,
                    vec.reshape(model_width, vec_width).astype(jnp.bfloat16),
                ],
                axis=1,
            )
        )
    attn_grad = jnp.stack(attn_grads).astype(jnp.float32)
    mlp_grad = jnp.stack(mlp_grads).astype(jnp.float32)
    vec = attn_grad[:, :, attn_width:].reshape(layers, -1)
    six = jnp.sum(lax.all_gather(vec[:, : vec_sizes[0]], "tp", axis=0, tiled=False), axis=0)
    six = six.reshape(layers, 6, shard_rows)
    edge = vec_sizes[0] + vec_sizes[1]
    return (
        stream.astype(jnp.bfloat16)[None],
        gradient[None],
        six[:, 0],
        six[:, 1],
        attn_grad[:, :, :qkv_width].reshape(w_qkv.shape),
        vec[:, vec_sizes[0] : edge].reshape(b_qv.shape),
        attn_grad[:, :, qkv_width:attn_width].swapaxes(1, 2),
        six[:, 2],
        six[:, 3],
        six[:, 4],
        mlp_grad[:, :, :hidden_width],
        vec[:, edge:vec_total].reshape(b_up.shape),
        mlp_grad[:, :, hidden_width:].swapaxes(1, 2),
        six[:, 5],
    )


def solution(mesh):
    in_specs = (
        P("dp", ("ctx", "tp"), None),
        P("dp", None),
        P(None, "dp"),
        P(None, "dp"),
        P(None, "dp", None, "tp"),
        P(None, None, "tp", "dp"),
        P(None, "tp", "dp"),
        P(None, "dp"),
        P(None, "dp"),
        P(None, "dp"),
        P(None, "dp", "tp"),
        P(None, "tp", "dp"),
        P(None, "tp", "dp"),
        P(None, "dp"),
        P("dp", ("ctx", "tp"), None),
    )
    out_specs = (
        P("dp", ("ctx", "tp"), None),
        P("dp", ("ctx", "tp"), None),
        P(None, "dp"),
        P(None, "dp"),
        P(None, "dp", None, "tp"),
        P(None, None, "tp", "dp"),
        P(None, "tp", "dp"),
        P(None, "dp"),
        P(None, "dp"),
        P(None, "dp"),
        P(None, "dp", "tp"),
        P(None, "tp", "dp"),
        P(None, "tp", "dp"),
        P(None, "dp"),
    )
    return jax.shard_map(body, mesh=mesh, in_specs=in_specs, out_specs=out_specs, check_vma=False)
```

```python
import functools

import jax
import jax.numpy as jnp
from jax import lax
from jax.experimental import pallas as pl
from jax.experimental.pallas import tpu as pltpu
from jax.sharding import PartitionSpec as P

HD = 64


def shifted_2(block, axis, distance):
    devices = range(lax.axis_size(axis))
    route = [(i - distance, i) for i in devices if i - distance in devices]
    return lax.ppermute(block, axis, route)


def normalize(stream, gain, shift):
    centered = stream - jnp.mean(stream, axis=-1, keepdims=True)
    inverse = lax.rsqrt(jnp.mean(centered * centered, axis=-1, keepdims=True) + 1e-05)
    unit_rows = centered * inverse
    return (unit_rows * gain + shift, unit_rows, inverse)


def normalize_back(gradient, unit_rows, inverse, gain):
    d_unit = gradient * gain
    d_stream = inverse * (
        d_unit
        - jnp.mean(d_unit, axis=-1, keepdims=True)
        - unit_rows * jnp.mean(d_unit * unit_rows, axis=-1, keepdims=True)
    )
    return (d_stream, jnp.sum(gradient * unit_rows, axis=0), jnp.sum(gradient, axis=0))


def contract_rows(left, right):
    return lax.dot_general(
        left, right, (((0,), (0,)), ((), ())), preferred_element_type=jnp.float32
    )


def contract_cols(left, right):
    return lax.dot_general(
        left, right, (((1,), (1,)), ((), ())), preferred_element_type=jnp.float32
    )


def greet(sibling, other):
    barrier = pltpu.get_barrier_semaphore()
    for peer in (sibling, other):
        pl.semaphore_signal(
            barrier, inc=1, device_id={"tp": peer}, device_id_type=pl.DeviceIdType.MESH
        )
    pl.semaphore_wait(barrier, 2)


def sent(source, target, send_sem, recv_sem, at, peer):
    return pltpu.make_async_remote_copy(
        src_ref=source,
        dst_ref=target,
        send_sem=send_sem.at[at],
        recv_sem=recv_sem.at[at],
        device_id={"tp": peer},
        device_id_type=pl.DeviceIdType.MESH,
    )


def quad():
    me = lax.axis_index("tp")
    return me, me + 1 - 2 * lax.rem(me, 2), lax.rem(me + 2, 4)


def rows_kernel(own_ref, all_ref, send_sem, recv_sem):
    me, sibling, other = quad()
    greet(sibling, other)
    over = sent(own_ref, all_ref.at[me], send_sem, recv_sem, 0, other)
    beside = sent(own_ref, all_ref.at[me], send_sem, recv_sem, 1, sibling)
    over.start()
    beside.start()
    all_ref[me] = own_ref[...]
    over.wait_recv()
    onward = sent(all_ref.at[other], all_ref.at[other], send_sem, recv_sem, 2, sibling)
    onward.start()
    beside.wait_recv()
    onward.wait_recv()
    over.wait_send()
    beside.wait_send()
    onward.wait_send()


def sums_kernel(term_ref, total_ref, landed, joint, send_sem, recv_sem):
    me, sibling, other = quad()
    far = lax.rem(sibling + 2, 4)
    greet(sibling, other)
    first = sent(term_ref.at[far], landed.at[0], send_sem, recv_sem, 0, sibling)
    second = sent(term_ref.at[sibling], landed.at[1], send_sem, recv_sem, 1, sibling)
    first.start()
    second.start()
    first.wait_recv()
    joint[...] = (
        term_ref[other].astype(jnp.float32) + landed[0].astype(jnp.float32)
    ).astype(jnp.bfloat16)
    over = sent(joint, landed.at[2], send_sem, recv_sem, 2, other)
    over.start()
    second.wait_recv()
    total_ref[...] = term_ref[me].astype(jnp.float32) + landed[1].astype(jnp.float32)
    over.wait_recv()
    total_ref[...] += landed[2].astype(jnp.float32)
    first.wait_send()
    second.wait_send()
    over.wait_send()


def gather_rows(local_rows):
    count = lax.axis_size("tp")
    if count != 4:
        return lax.all_gather(local_rows, "tp", axis=0, tiled=True)
    wide = pl.pallas_call(
        rows_kernel,
        out_shape=jax.ShapeDtypeStruct((count,) + local_rows.shape, local_rows.dtype),
        in_specs=[pl.BlockSpec(memory_space=pltpu.VMEM)],
        out_specs=pl.BlockSpec(memory_space=pltpu.VMEM),
        scratch_shapes=[pltpu.SemaphoreType.DMA((3,)), pltpu.SemaphoreType.DMA((3,))],
        compiler_params=pltpu.CompilerParams(collective_id=1, has_side_effects=True),
    )(local_rows)
    return wide.reshape(count * local_rows.shape[0], local_rows.shape[1])


def scatter_rows(term):
    count = lax.axis_size("tp")
    blocks = term.astype(jnp.bfloat16).reshape(count, term.shape[0] // count, term.shape[1])
    if count != 4:
        landed = lax.all_to_all(blocks, "tp", split_axis=0, concat_axis=0)
        return jnp.sum(landed.astype(jnp.float32), axis=0)
    block = blocks.shape[1:]
    return pl.pallas_call(
        sums_kernel,
        out_shape=jax.ShapeDtypeStruct(block, jnp.float32),
        in_specs=[pl.BlockSpec(memory_space=pltpu.VMEM)],
        out_specs=pl.BlockSpec(memory_space=pltpu.VMEM),
        scratch_shapes=[
            pltpu.VMEM((3,) + block, jnp.bfloat16),
            pltpu.VMEM(block, jnp.bfloat16),
            pltpu.SemaphoreType.DMA((3,)),
            pltpu.SemaphoreType.DMA((3,)),
        ],
        compiler_params=pltpu.CompilerParams(collective_id=2, has_side_effects=True),
    )(blocks)


def swapped(block):
    return lax.ppermute(block, "ctx", [(0, 1), (1, 0)])


def rotated(block, distance):
    count = lax.axis_size("dp")
    return lax.ppermute(block, "dp", [(i, (i + distance) % count) for i in range(count)])


def gather_kernel(count, pieces, *refs):
    ins, outs = refs[:pieces], refs[pieces : 2 * pieces]
    line_send, line_recv, side_send, side_recv, own_sem = refs[2 * pieces :]
    me, side = lax.axis_index("dp"), lax.axis_index("ctx")
    barrier = pltpu.get_barrier_semaphore()
    pl.semaphore_signal(
        barrier, inc=1, device_id={"ctx": 1 - side}, device_id_type=pl.DeviceIdType.MESH
    )
    for way in (1, -1):

        @pl.when((me + way >= 0) & (me + way < count))
        def _():
            pl.semaphore_signal(
                barrier, inc=1, device_id={"dp": me + way}, device_id_type=pl.DeviceIdType.MESH
            )

    ends = jnp.where(me == 0, 1, 0) + jnp.where(me == count - 1, 1, 0)
    pl.semaphore_wait(barrier, 3 - ends)

    def line(piece, turn, step):
        way = 1 - 2 * turn
        owner = me - way * (step - 1)
        source = ins[piece].at[side] if step == 1 else outs[piece].at[owner, side]
        return pltpu.make_async_remote_copy(
            src_ref=source,
            dst_ref=outs[piece].at[owner, side],
            send_sem=line_send.at[piece, turn, step - 1],
            recv_sem=line_recv.at[piece, turn, step - 1],
            device_id={"dp": me + way},
            device_id_type=pl.DeviceIdType.MESH,
        )

    def arriving(piece, turn, step):
        owner = me - (1 - 2 * turn) * step
        return pltpu.make_async_remote_copy(
            src_ref=ins[piece].at[side],
            dst_ref=outs[piece].at[owner, side],
            send_sem=line_send.at[piece, turn, step - 1],
            recv_sem=line_recv.at[piece, turn, step - 1],
            device_id={"ctx": 1 - side},
            device_id_type=pl.DeviceIdType.MESH,
        )

    def across(piece, turn, step, half):
        owner = me - (1 - 2 * turn) * step
        return pltpu.make_async_remote_copy(
            src_ref=outs[piece].at[owner, half],
            dst_ref=outs[piece].at[owner, half],
            send_sem=side_send.at[piece, turn, step - 1],
            recv_sem=side_recv.at[piece, turn, step - 1],
            device_id={"ctx": 1 - side},
            device_id_type=pl.DeviceIdType.MESH,
        )

    def sends(turn, step):
        way = 1 - 2 * turn
        owner = me - way * (step - 1)
        return (owner >= 0) & (owner < count) & (me + way >= 0) & (me + way < count)

    def lands(turn, step):
        owner = me - (1 - 2 * turn) * step
        return (owner >= 0) & (owner < count)

    def own(piece):
        return pltpu.make_async_copy(ins[piece], outs[piece].at[me], own_sem.at[piece])

    for piece in range(pieces):
        for turn in (0, 1):

            @pl.when(sends(turn, 1))
            def _():
                line(piece, turn, 1).start()

    for piece in range(pieces):
        own(piece).start()
    for step in range(1, count):
        for piece in range(pieces):
            for turn in (0, 1):

                @pl.when(lands(turn, step))
                def _():
                    arriving(piece, turn, step).wait_recv()
                    across(piece, turn, step, side).start()

                if step + 1 < count:

                    @pl.when(sends(turn, step + 1))
                    def _():
                        line(piece, turn, step + 1).start()

    for step in range(1, count):
        for piece in range(pieces):
            for turn in (0, 1):

                @pl.when(lands(turn, step))
                def _():
                    across(piece, turn, step, side).wait_send()
                    across(piece, turn, step, 1 - side).wait_recv()

                @pl.when(sends(turn, step))
                def _():
                    line(piece, turn, step).wait_send()

    for piece in range(pieces):
        own(piece).wait()


def gather_shards(shards):
    count = lax.axis_size("dp")
    pieces = len(shards)
    padded = []
    for shard in shards:
        pad = -shard.shape[0] % 32
        shard = jnp.pad(shard, ((0, pad), (0, 0))) if pad else shard
        padded.append(shard.reshape(2, shard.shape[0] // 2, shard.shape[1]))
    steps = (pieces, 2, max(count - 1, 1))
    landed = pl.pallas_call(
        functools.partial(gather_kernel, count, pieces),
        out_shape=[jax.ShapeDtypeStruct((count,) + item.shape, item.dtype) for item in padded],
        in_specs=[pl.BlockSpec(memory_space=pl.ANY)] * pieces,
        out_specs=[pl.BlockSpec(memory_space=pl.ANY)] * pieces,
        scratch_shapes=[pltpu.SemaphoreType.DMA(steps)] * 4 + [pltpu.SemaphoreType.DMA((pieces,))],
        compiler_params=pltpu.CompilerParams(collective_id=0, has_side_effects=True),
    )(*padded)
    return [
        item.reshape(count, -1, item.shape[-1])[:, : shard.shape[0]]
        for item, shard in zip(landed, shards)
    ]


def reduce_split(whole):
    count, me, side = lax.axis_size("dp"), lax.axis_index("dp"), lax.axis_index("ctx")
    rows, width = whole.shape[0] // count, whole.shape[1]
    half = rows // 2
    blocks = whole.reshape(count, 2, half, width)
    theirs = lax.dynamic_index_in_dim(blocks, 1 - side, 1, keepdims=False)
    mine = lax.dynamic_index_in_dim(blocks, side, 1, keepdims=False)
    both = (mine.astype(jnp.float32) + swapped(theirs).astype(jnp.float32)).astype(jnp.bfloat16)
    total = lax.dynamic_index_in_dim(both, me, 0, keepdims=False).astype(jnp.float32)
    for k in range(1, count):
        block = lax.dynamic_index_in_dim(both, lax.rem(me + k, count), 0, keepdims=False)
        total = total + rotated(block, k).astype(jnp.float32)
    total = total.astype(jnp.bfloat16)
    other = swapped(total)
    return jnp.concatenate(
        [jnp.where(side == 0, total, other), jnp.where(side == 0, other, total)], axis=0
    )


def batched(left, right, left_dim, right_dim):
    return lax.dot_general(
        left, right, (((left_dim,), (right_dim,)), ((0,), (0,))), preferred_element_type=jnp.float32
    )


def masked_scores(query_rows, key_rows, visible):
    scores = batched(query_rows, key_rows, 1, 1) * HD ** (-0.5)
    return jnp.where(visible[None], scores, -1e30)


def attend(query_rows, key_rows, value_rows, visible):
    scores = masked_scores(query_rows, key_rows, visible)
    row_max = jnp.max(scores, axis=-1)
    shifted = jnp.exp(scores - row_max[..., None])
    row_total = jnp.sum(shifted, axis=-1)
    soft_rows = (shifted / row_total[..., None]).astype(jnp.bfloat16)
    mixed = batched(value_rows, soft_rows, 2, 2)
    return (mixed, row_max + jnp.log(row_total))


def attend_back(query_rows, key_rows, value_rows, log_total, d_mixed, visible):
    scores = masked_scores(query_rows, key_rows, visible)
    soft_rows = jnp.exp(scores - log_total[..., None])
    d_soft = batched(d_mixed, value_rows, 1, 1)
    row_dot = jnp.sum(soft_rows * d_soft, axis=-1)
    d_scores = (soft_rows * (d_soft - row_dot[..., None])).astype(jnp.bfloat16)
    d_query = batched(key_rows, d_scores, 2, 2) * HD ** (-0.5)
    d_keys = batched(query_rows, d_scores, 2, 1) * HD ** (-0.5)
    d_values = batched(d_mixed, soft_rows.astype(jnp.bfloat16), 2, 1)
    return (d_query, d_keys, d_values)


def body(
    inputs,
    segments,
    ln1_gain,
    ln1_shift,
    w_qkv,
    b_qv,
    w_out,
    b_out,
    ln2_gain,
    ln2_shift,
    w_up,
    b_up,
    w_down,
    b_down,
    cotangent,
):
    tp_count = lax.axis_size("tp")
    dp_count = lax.axis_size("dp")
    pair_index = lax.axis_index("ctx")
    row_count = inputs.shape[1]
    group_rows = row_count * tp_count
    model_width = inputs.shape[2]
    layers = ln1_gain.shape[0]
    shard_rows = ln1_gain.shape[1]
    heads_width = w_qkv.shape[3]
    hidden_width = w_up.shape[2]
    head_count, head_part = b_qv.shape[2], b_qv.shape[3]
    unit_rows_up = b_up.shape[1]
    qkv_width = 3 * heads_width
    attn_width = qkv_width + heads_width
    head_shape = (heads_width // HD, HD, group_rows)
    vec_sizes = [6 * shard_rows, 2 * head_count * head_part, unit_rows_up * head_part]
    vec_total = sum(vec_sizes)
    vec_width = 128 * (-(-vec_total // (128 * shard_rows)))

    query_pos = pair_index * group_rows + jnp.arange(group_rows, dtype=jnp.int32)
    key_pos = (pair_index - 1) * group_rows + jnp.arange(2 * group_rows, dtype=jnp.int32)
    padded_ids = jnp.concatenate([jnp.full((group_rows,), -1, jnp.int32), segments[0]])
    key_ids = lax.dynamic_slice_in_dim(padded_ids, pair_index * group_rows, 2 * group_rows)
    query_ids = lax.dynamic_slice_in_dim(segments[0], pair_index * group_rows, group_rows)
    visible = (key_pos[None, :] <= query_pos[:, None]) & (key_ids[None, :] == query_ids[:, None])

    def pack_vec(rows_six, bias_qv, bias_up):
        lead = rows_six.shape[:-1]
        flat = jnp.concatenate([rows_six, bias_qv, bias_up], axis=-1)
        pad = shard_rows * vec_width - vec_total
        flat = jnp.pad(flat, [(0, 0)] * len(lead) + [(0, pad)])
        return flat.reshape(lead + (shard_rows, vec_width))

    shards = []
    for layer in range(layers):
        shards.append(
            jnp.concatenate(
                [w_qkv[layer].reshape(shard_rows, qkv_width), w_out[layer].T], axis=1
            )
        )
        shards.append(jnp.concatenate([w_up[layer], w_down[layer].T], axis=1))
    side_width = 128 * (-(-max(shard_rows, head_part) // 128))
    vec_rows = []
    for member in (ln1_gain, ln1_shift, b_out, ln2_gain, ln2_shift, b_down, b_qv, b_up):
        flat = member.reshape(-1, member.shape[-1])
        vec_rows.append(jnp.pad(flat, ((0, 0), (0, side_width - flat.shape[1]))))
    shards.append(jnp.concatenate(vec_rows, axis=0))
    landed = gather_shards(shards)
    vecs = landed[-1].astype(jnp.float32)
    edge_six, edge_qv = 6 * layers, 6 * layers + 2 * layers * head_count

    def widened(start, stop, width):
        return jnp.concatenate([vecs[i, start:stop, :width] for i in range(dp_count)], axis=1)

    all_six = widened(0, edge_six, shard_rows)
    all_qv = widened(edge_six, edge_qv, head_part).reshape(layers, 2, head_count, HD)
    all_up = widened(edge_qv, edge_qv + layers * unit_rows_up, head_part)
    all_up = all_up.reshape(layers, hidden_width)

    stream = inputs[0].astype(jnp.float32)
    saved = []
    for layer in range(layers):
        attn_all = landed[2 * layer].reshape(model_width, attn_width)
        mlp_all = landed[2 * layer + 1].reshape(model_width, 2 * hidden_width)
        qkv_weight = attn_all[:, :qkv_width]
        out_flipped = attn_all[:, qkv_width:attn_width]
        up_weight = mlp_all[:, :hidden_width]
        down_flipped = mlp_all[:, hidden_width:]
        gain_one, shift_one, out_bias, gain_two, shift_two, down_bias = [
            all_six[member * layers + layer] for member in range(6)
        ]
        up_bias = all_up[layer]
        normed, unit_one, inverse_one = normalize(stream, gain_one, shift_one)
        hidden_attn = gather_rows(normed.astype(jnp.bfloat16))
        projected = lax.dot_general(
            qkv_weight,
            hidden_attn,
            (((0,), (1,)), ((), ())),
            preferred_element_type=jnp.float32,
        ).reshape((3,) + head_shape)
        query_rows = (projected[0] + all_qv[layer, 0][:, :, None]).astype(jnp.bfloat16)
        key_rows = projected[1].astype(jnp.bfloat16)
        value_rows = (projected[2] + all_qv[layer, 1][:, :, None]).astype(jnp.bfloat16)
        earlier_keys, earlier_values = shifted_2((key_rows, value_rows), "ctx", 1)
        all_keys = jnp.concatenate([earlier_keys, key_rows], axis=2)
        all_values = jnp.concatenate([earlier_values, value_rows], axis=2)
        mixed, log_total = attend(query_rows, all_keys, all_values, visible)
        mixed = mixed.reshape(heads_width, group_rows).astype(jnp.bfloat16)
        out_term = lax.dot_general(
            mixed, out_flipped, (((0,), (1,)), ((), ())), preferred_element_type=jnp.float32
        )
        stream_mid = stream + scatter_rows(out_term) + out_bias
        normed_two, unit_two, inverse_two = normalize(stream_mid, gain_two, shift_two)
        hidden_mlp = gather_rows(normed_two.astype(jnp.bfloat16))
        upper = jnp.dot(hidden_mlp, up_weight, preferred_element_type=jnp.float32) + up_bias
        acts = jax.nn.gelu(upper).astype(jnp.bfloat16)
        stream = stream_mid + scatter_rows(contract_cols(acts, down_flipped)) + down_bias
        saved.append(
            (
                qkv_weight,
                out_flipped,
                up_weight,
                down_flipped,
                gain_one,
                gain_two,
                unit_one,
                inverse_one,
                hidden_attn,
                query_rows,
                all_keys,
                all_values,
                log_total,
                mixed,
                unit_two,
                inverse_two,
                hidden_mlp,
                upper,
                acts,
            )
        )
    gradient = cotangent[0].astype(jnp.float32)
    attn_grads, mlp_grads = [None] * layers, [None] * layers
    for layer in reversed(range(layers)):
        (
            qkv_weight,
            out_flipped,
            up_weight,
            down_flipped,
            gain_one,
            gain_two,
            unit_one,
            inverse_one,
            hidden_attn,
            query_rows,
            all_keys,
            all_values,
            log_total,
            mixed,
            unit_two,
            inverse_two,
            hidden_mlp,
            upper,
            acts,
        ) = saved[layer]
        g_mlp = gradient.astype(jnp.bfloat16)
        d_down_bias = jnp.sum(g_mlp.astype(jnp.float32), axis=0)
        wide_mlp = gather_rows(g_mlp)
        d_acts = jnp.dot(wide_mlp, down_flipped, preferred_element_type=jnp.float32)
        gelu_pull = jax.vjp(jax.nn.gelu, upper)[1]
        d_upper = gelu_pull(d_acts)[0].astype(jnp.bfloat16)
        d_norm_two = scatter_rows(contract_cols(d_upper, up_weight))
        d_up_bias = jnp.sum(d_upper.astype(jnp.float32), axis=0)
        mlp_grads[layer] = reduce_split(
            jnp.concatenate(
                [
                    contract_rows(hidden_mlp, d_upper).astype(jnp.bfloat16),
                    contract_rows(wide_mlp, acts).astype(jnp.bfloat16),
                ],
                axis=1,
            )
        )
        d_mid, d_gain_two, d_shift_two = normalize_back(d_norm_two, unit_two, inverse_two, gain_two)
        gradient_mid = gradient + d_mid
        g_attn = gradient_mid.astype(jnp.bfloat16)
        d_out_bias = jnp.sum(g_attn.astype(jnp.float32), axis=0)
        wide_attn = gather_rows(g_attn)
        d_out_flipped = lax.dot_general(
            wide_attn, mixed, (((0,), (1,)), ((), ())), preferred_element_type=jnp.float32
        ).astype(jnp.bfloat16)
        d_mixed = (
            lax.dot_general(
                out_flipped, wide_attn, (((0,), (1,)), ((), ())), preferred_element_type=jnp.float32
            )
            .astype(jnp.bfloat16)
            .reshape(head_shape)
        )
        d_query, d_keys, d_values = attend_back(
            query_rows, all_keys, all_values, log_total, d_mixed, visible
        )
        later_keys, later_values = shifted_2(
            (
                d_keys[:, :, :group_rows].astype(jnp.bfloat16),
                d_values[:, :, :group_rows].astype(jnp.bfloat16),
            ),
            "ctx",
            -1,
        )
        d_query = d_query.astype(jnp.bfloat16).reshape(heads_width, group_rows)
        d_key_own = (
            (d_keys[:, :, group_rows:] + later_keys.astype(jnp.float32))
            .astype(jnp.bfloat16)
            .reshape(heads_width, group_rows)
        )
        d_value_own = (
            (d_values[:, :, group_rows:] + later_values.astype(jnp.float32))
            .astype(jnp.bfloat16)
            .reshape(heads_width, group_rows)
        )
        d_projected = jnp.concatenate([d_query, d_key_own, d_value_own], axis=0)
        d_norm_one = scatter_rows(
            lax.dot_general(
                d_projected, qkv_weight, (((0,), (1,)), ((), ())), preferred_element_type=jnp.float32
            )
        )
        d_qkv_weight = lax.dot_general(
            hidden_attn, d_projected, (((0,), (1,)), ((), ())), preferred_element_type=jnp.float32
        ).astype(jnp.bfloat16)
        d_qv_bias = jnp.stack(
            [
                jnp.sum(d_query.astype(jnp.float32), axis=1),
                jnp.sum(d_value_own.astype(jnp.float32), axis=1),
            ]
        )
        d_input, d_gain_one, d_shift_one = normalize_back(
            d_norm_one, unit_one, inverse_one, gain_one
        )
        gradient = gradient_mid + d_input
        six = jnp.stack(
            [d_gain_one, d_shift_one, d_out_bias, d_gain_two, d_shift_two, d_down_bias]
        ).reshape(6, dp_count, shard_rows)
        vec = pack_vec(
            six.swapaxes(0, 1).reshape(dp_count, -1),
            d_qv_bias.reshape(2 * head_count, dp_count, head_part)
            .swapaxes(0, 1)
            .reshape(dp_count, -1),
            d_up_bias.reshape(unit_rows_up, dp_count, head_part)
            .swapaxes(0, 1)
            .reshape(dp_count, -1),
        )
        attn_grads[layer] = reduce_split(
            jnp.concatenate(
                [
                    d_qkv_weight,
                    d_out_flipped,
                    vec.reshape(model_width, vec_width).astype(jnp.bfloat16),
                ],
                axis=1,
            )
        )
    attn_grad = jnp.stack(attn_grads).astype(jnp.float32)
    mlp_grad = jnp.stack(mlp_grads).astype(jnp.float32)
    vec = attn_grad[:, :, attn_width:].reshape(layers, -1)
    six = jnp.sum(lax.all_gather(vec[:, : vec_sizes[0]], "tp", axis=0, tiled=False), axis=0)
    six = six.reshape(layers, 6, shard_rows)
    edge = vec_sizes[0] + vec_sizes[1]
    return (
        stream.astype(jnp.bfloat16)[None],
        gradient[None],
        six[:, 0],
        six[:, 1],
        attn_grad[:, :, :qkv_width].reshape(w_qkv.shape),
        vec[:, vec_sizes[0] : edge].reshape(b_qv.shape),
        attn_grad[:, :, qkv_width:attn_width].swapaxes(1, 2),
        six[:, 2],
        six[:, 3],
        six[:, 4],
        mlp_grad[:, :, :hidden_width],
        vec[:, edge:vec_total].reshape(b_up.shape),
        mlp_grad[:, :, hidden_width:].swapaxes(1, 2),
        six[:, 5],
    )


def solution(mesh):
    in_specs = (
        P("dp", ("ctx", "tp"), None),
        P("dp", None),
        P(None, "dp"),
        P(None, "dp"),
        P(None, "dp", None, "tp"),
        P(None, None, "tp", "dp"),
        P(None, "tp", "dp"),
        P(None, "dp"),
        P(None, "dp"),
        P(None, "dp"),
        P(None, "dp", "tp"),
        P(None, "tp", "dp"),
        P(None, "tp", "dp"),
        P(None, "dp"),
        P("dp", ("ctx", "tp"), None),
    )
    out_specs = (
        P("dp", ("ctx", "tp"), None),
        P("dp", ("ctx", "tp"), None),
        P(None, "dp"),
        P(None, "dp"),
        P(None, "dp", None, "tp"),
        P(None, None, "tp", "dp"),
        P(None, "tp", "dp"),
        P(None, "dp"),
        P(None, "dp"),
        P(None, "dp"),
        P(None, "dp", "tp"),
        P(None, "tp", "dp"),
        P(None, "tp", "dp"),
        P(None, "dp"),
    )
    return jax.shard_map(body, mesh=mesh, in_specs=in_specs, out_specs=out_specs, check_vma=False)
```
